32 devices in a mesh: dp: 4 (over y, x), ctx: 8 (over z, core).
Axes of the slice: x: 2, y: 2, z: 4, core: 2. Of those that a mesh axis runs over, the one named last changes fastest.
Arguments:
- queries: bfloat16 [4, 2048, 512], P('dp', 'ctx'), may hold values from -6 to 6
- key_vectors: bfloat16 [4, 2048, 512], P('dp', 'ctx'), may hold values from -6 to 6
- value_vectors: bfloat16 [4, 2048, 512], P('dp', 'ctx'), may hold values from -6 to 6
- grad_output: bfloat16 [4, 2048, 512], P('dp', 'ctx'), may hold values from -768 to 768
- pattern: int32 [4, 16, 2], P('dp', 'ctx'), may hold values from 0 to 1
- lengths: int32 [4, 1], P('dp'), may hold values from 512 to 2048, as said below
- widths: int32 [4, 1], P('dp'), may hold values from 1 to 2, as said below
- relative_bucket_bias: float32 [4, 7], replicated, may hold values from -4 to 4
Outputs:
- grad_queries: bfloat16 [4, 2048, 512], P('dp', 'ctx')
- grad_keys: bfloat16 [4, 2048, 512], P('dp', 'ctx')
- value_row_gradients: bfloat16 [4, 2048, 512], P('dp', 'ctx')
- grad_bias: float32 [4, 7], replicated
The draws below stay inside these ranges and needn't reach their ends.
Inputs may be any that keep to these rules, and one draw needn't show every extreme that they name: `lengths`: one user has a history of all 2048 events and one has 512. `widths`: some user has the widest band and some the narrowest.
All inputs are finite; a program needn't handle non-finite values.
Results may differ from the reference program's by a relative error of at most 0.005.
Values may be sent and summed in bfloat16 or wider, within the bound.
A program may use at most 64 MiB of HBM per device.

```python
import jax
import jax.numpy as jnp
from jax import lax

D = 512
HEADS = 4
BLOCK = 128
GROUP = 8
FAR = 2
NBUCK = 7
TOK_DEV = 256
BLK_DEV = 2
SEQ = 2048
N_DP = 4
N_CTX = 8


def draw_lengths(key, part):
    values = jax.random.randint(key, (N_DP, N_CTX // GROUP), SEQ // 4, SEQ + 1, dtype=jnp.int32)
    values = values.at[0, 0].set(SEQ)
    return values.at[N_DP - 1, N_CTX // GROUP - 1].set(SEQ // 4)


def draw_widths(key, part):
    values = jax.random.randint(jax.random.fold_in(key, 7), (N_DP, N_CTX // GROUP), 1, BLK_DEV + 1, dtype=jnp.int32)
    values = values.at[0, 0].set(BLK_DEV)
    return values.at[N_DP - 1, N_CTX // GROUP - 1].set(1)


def touch_ends(values, key, smallest, top_value):
    index_at = [jax.random.randint(jax.random.fold_in(key, axis), (), 0, length) for axis, length in enumerate(values.shape)]
    longest = values.shape.index(max(values.shape))
    neighbour = index_at[:longest] + [(index_at[longest] + 1) % values.shape[longest]] + index_at[longest + 1:]
    return values.at[tuple(index_at)].set(smallest).at[tuple(neighbour)].set(top_value)


def shard_levels(own_key, dims, shards, least, largest):
    level = 1.0
    for dim, shards_of in shards:
        steps = jax.random.uniform(jax.random.fold_in(jax.random.fold_in(own_key, 6), dim), (shards_of,), jnp.float32, least / len(shards), largest / len(shards))
        level = level * jnp.repeat(jnp.exp(steps), dims[dim] // shards_of).reshape((-1,) + (1,) * (len(dims) - 1 - dim))
    return level


def gaussian(own_key, shape, spread, limit, split=(), kind=jnp.bfloat16):
    values = spread * jax.random.normal(own_key, shape, jnp.float32)
    if split:
        values = values * shard_levels(own_key, shape, split, -0.22, 0.18)
    return jnp.clip(values, -limit, limit).astype(kind)


def setup_inputs(seed: int = 0) -> dict:
    key_of = jax.random.split(jax.random.key(seed), 9)
    return {
        "queries": gaussian(key_of[0], (N_DP, N_CTX * TOK_DEV, D), 1.0, 6.0, ((0, 4), (1, 8))),
        "key_vectors": gaussian(key_of[1], (N_DP, N_CTX * TOK_DEV, D), 1.0, 6.0, ((0, 4), (1, 8))),
        "value_vectors": gaussian(key_of[2], (N_DP, N_CTX * TOK_DEV, D), 1.0, 6.0, ((0, 4), (1, 8))),
        "grad_output": gaussian(key_of[3], (N_DP, N_CTX * TOK_DEV, D), (SEQ / 16), 768.0, ((0, 4), (1, 8))),
        "pattern": touch_ends(jax.random.randint(key_of[4], (N_DP, N_CTX * BLK_DEV, FAR), 0, BLK_DEV), jax.random.fold_in(key_of[4], 1), 0, BLK_DEV - 1).astype(jnp.int32),
        "lengths": draw_lengths(jax.random.fold_in(key_of[8], 71), 0),
        "widths": draw_widths(jax.random.fold_in(key_of[8], 71), 0),
        "relative_bucket_bias": gaussian(key_of[7], (HEADS, NBUCK), 1.0, 4.0, (), jnp.float32),
    }


def tile_grads(q_rows, g_rows, k_rows, v_rows, keep_mask, buckets, relative_bucket_bias):
    groups, query_len, model_width = q_rows.shape
    key_len = k_rows.shape[1]
    head_count = relative_bucket_bias.shape[0]
    head_dim = model_width // head_count
    q_blocks = query_len // BLOCK
    k_blocks = key_len // BLOCK
    scaling = head_dim ** -0.5
    q_heads = q_rows.astype(jnp.float32).reshape(groups, query_len, head_count, head_dim)
    g_heads = g_rows.astype(jnp.float32).reshape(groups, query_len, head_count, head_dim)
    k_heads = k_rows.astype(jnp.float32).reshape(groups, key_len, head_count, head_dim)
    v_heads = v_rows.astype(jnp.float32).reshape(groups, key_len, head_count, head_dim)
    raw_score = jnp.einsum("gqhd,gkhd->ghqk", q_heads, k_heads)
    onehot = (buckets[..., None] == jnp.arange(NBUCK, dtype=jnp.int32)).astype(jnp.float32)
    bias_tile = jnp.einsum("gxyu,hu->ghxy", onehot, relative_bucket_bias, precision=lax.Precision.HIGHEST)
    score = (raw_score * scaling).reshape(groups, head_count, q_blocks, BLOCK, k_blocks, BLOCK)
    score = (score + bias_tile[:, :, :, None, :, None]).reshape(groups, head_count, query_len, key_len)
    sigmoid_s = jax.nn.sigmoid(score)
    factor = keep_mask[:, None, :, :] / SEQ
    weights_bf = (score * sigmoid_s * factor).astype(jnp.bfloat16)
    weights_bf = lax.optimization_barrier(weights_bf).astype(jnp.float32)
    value_gradient = jnp.einsum("ghqk,gqhd->gkhd", weights_bf, g_heads)
    grad_prob = jnp.einsum("gqhd,gkhd->ghqk", g_heads, v_heads)
    dscore = grad_prob * (sigmoid_s * (1.0 + score * (1.0 - sigmoid_s))) * factor
    block_sums = dscore.reshape(groups, head_count, q_blocks, BLOCK, k_blocks, BLOCK).sum(axis=(3, 5))
    grad_bias = jnp.einsum("ghxy,gxyu->hu", block_sums, onehot, precision=lax.Precision.HIGHEST)
    dscore_bf = lax.optimization_barrier(dscore.astype(jnp.bfloat16)).astype(jnp.float32)
    grad_q = jnp.einsum("ghqk,gkhd->gqhd", dscore_bf, k_heads) * scaling
    key_gradient = jnp.einsum("ghqk,gqhd->gkhd", dscore_bf, q_heads) * scaling
    return (grad_q.reshape(groups, query_len, model_width), key_gradient.reshape(groups, key_len, model_width),
            value_gradient.reshape(groups, key_len, model_width), grad_bias)


def local_mask(span_id, length, band_width, token_count):
    blocks = token_count // BLOCK
    places = span_id * token_count + jnp.arange(token_count, dtype=jnp.int32)
    block_ids = jnp.arange(token_count, dtype=jnp.int32) // BLOCK
    allowed = (block_ids[:, None] - block_ids[None, :] <= band_width) & (places[None, :] <= places[:, None])
    allowed = allowed & (places[:, None] < length) & (places[None, :] < length)
    grid = jnp.arange(blocks, dtype=jnp.int32)
    buckets = jnp.clip(grid[:, None] - grid[None, :], 0, NBUCK - 1)
    return allowed.astype(jnp.float32)[None], buckets[None]


def near_mask(span_id, length, band_width, token_count):
    blocks = token_count // BLOCK
    q_places = span_id * token_count + jnp.arange(token_count, dtype=jnp.int32)
    k_places = (span_id - 1) * token_count + jnp.arange(token_count, dtype=jnp.int32)
    block_ids = jnp.arange(token_count, dtype=jnp.int32) // BLOCK
    distance = block_ids[:, None] + blocks - block_ids[None, :]
    allowed = (distance <= band_width) & (q_places[:, None] < length) & (k_places[None, :] < length)
    allowed = allowed & (span_id >= 1) & (span_id < GROUP)
    grid = jnp.arange(blocks, dtype=jnp.int32)
    buckets = jnp.clip(grid[:, None] + blocks - grid[None, :], 0, NBUCK - 1)
    return allowed.astype(jnp.float32)[None], buckets[None]


def far_mask(span_id, chosen, distance, length, token_count):
    blocks = token_count // BLOCK
    grid = jnp.arange(blocks, dtype=jnp.int32)
    inner = jnp.arange(BLOCK, dtype=jnp.int32)
    q_places = span_id * token_count + grid[:, None] * BLOCK + inner[None, :]
    k_places = (span_id - distance) * token_count + chosen[:, None] * BLOCK + inner[None, :]
    allowed = (q_places[:, :, None] < length) & (k_places[:, None, :] < length)
    allowed = allowed & (span_id >= distance) & (span_id < GROUP)
    buckets = jnp.clip(distance * blocks + grid - chosen, 0, NBUCK - 1)[:, None, None]
    return allowed.astype(jnp.float32), buckets


def local_terms(q_rows, g_rows, k_rows, v_rows, span_id, length, band_width, relative_bucket_bias):
    keep_mask, buckets = local_mask(span_id, length, band_width, q_rows.shape[0])
    grads = tile_grads(q_rows[None], g_rows[None], k_rows[None], v_rows[None], keep_mask, buckets, relative_bucket_bias)
    return grads[0][0], grads[1][0], grads[2][0], grads[3]


def near_terms(q_rows, g_rows, k_rows, v_rows, span_id, length, band_width, relative_bucket_bias):
    keep_mask, buckets = near_mask(span_id, length, band_width, q_rows.shape[0])
    grads = tile_grads(q_rows[None], g_rows[None], k_rows[None], v_rows[None], keep_mask, buckets, relative_bucket_bias)
    return grads[0][0], grads[1][0], grads[2][0], grads[3]


def far_terms(q_rows, g_rows, k_rows, v_rows, chosen, span_id, distance, length, relative_bucket_bias):
    token_count, model_width = q_rows.shape
    blocks = token_count // BLOCK
    keep_mask, buckets = far_mask(span_id, chosen, distance, length, token_count)
    q_tiles = q_rows.reshape(blocks, BLOCK, model_width)
    g_tiles = g_rows.reshape(blocks, BLOCK, model_width)
    k_tiles = jnp.take(k_rows.reshape(blocks, BLOCK, model_width), chosen, axis=0)
    v_tiles = jnp.take(v_rows.reshape(blocks, BLOCK, model_width), chosen, axis=0)
    grad_q, key_gradient, value_gradient, grad_bias = tile_grads(q_tiles, g_tiles, k_tiles, v_tiles, keep_mask, buckets, relative_bucket_bias)
    selector_matrix = (chosen[:, None] == jnp.arange(blocks, dtype=jnp.int32)[None, :]).astype(jnp.float32)
    key_gradient = jnp.einsum("as,apc->spc", selector_matrix, key_gradient, precision=lax.Precision.HIGHEST).reshape(token_count, model_width)
    value_gradient = jnp.einsum("as,apc->spc", selector_matrix, value_gradient, precision=lax.Precision.HIGHEST).reshape(token_count, model_width)
    return grad_q.reshape(token_count, model_width), key_gradient, value_gradient, grad_bias


def history_grads(query_history, g_hist, k_hist, v_hist, block_table, length, band_width, relative_bucket_bias):
    def part_of(source, span_id):
        return source[span_id * TOK_DEV:(span_id + 1) * TOK_DEV]

    empty_rows = jnp.zeros((TOK_DEV, D), jnp.float32)
    sum_q = [empty_rows] * GROUP
    sum_k = [empty_rows] * GROUP
    sum_v = [empty_rows] * GROUP
    bias_total = jnp.zeros((HEADS, NBUCK), jnp.float32)
    for span_id in range(GROUP):
        q_rows = part_of(query_history, span_id)
        g_rows = part_of(g_hist, span_id)
        terms = local_terms(q_rows, g_rows, part_of(k_hist, span_id), part_of(v_hist, span_id),
                            span_id, length, band_width, relative_bucket_bias)
        sum_q[span_id] = sum_q[span_id] + terms[0]
        sum_k[span_id] = sum_k[span_id] + terms[1]
        sum_v[span_id] = sum_v[span_id] + terms[2]
        bias_total = bias_total + terms[3]
        if span_id >= 1:
            terms = near_terms(q_rows, g_rows, part_of(k_hist, span_id - 1), part_of(v_hist, span_id - 1),
                               span_id, length, band_width, relative_bucket_bias)
            sum_q[span_id] = sum_q[span_id] + terms[0]
            sum_k[span_id - 1] = sum_k[span_id - 1] + terms[1]
            sum_v[span_id - 1] = sum_v[span_id - 1] + terms[2]
            bias_total = bias_total + terms[3]
        for far_level in range(FAR):
            distance = 2 ** (far_level + 1)
            if span_id >= distance:
                source_id = span_id - distance
                terms = far_terms(q_rows, g_rows, part_of(k_hist, source_id), part_of(v_hist, source_id),
                                  block_table[span_id][:, far_level], span_id, distance, length, relative_bucket_bias)
                sum_q[span_id] = sum_q[span_id] + terms[0]
                sum_k[source_id] = sum_k[source_id] + terms[1]
                sum_v[source_id] = sum_v[source_id] + terms[2]
                bias_total = bias_total + terms[3]
    return (jnp.concatenate(sum_q, axis=0).astype(jnp.bfloat16),
            jnp.concatenate(sum_k, axis=0).astype(jnp.bfloat16),
            jnp.concatenate(sum_v, axis=0).astype(jnp.bfloat16), bias_total)


def reference(queries, key_vectors, value_vectors, grad_output, pattern, lengths, widths, relative_bucket_bias):
    user_count = N_DP * (N_CTX // GROUP)
    q_all = queries.reshape(user_count, SEQ, D)
    g_all = grad_output.reshape(user_count, SEQ, D)
    k_all = key_vectors.reshape(user_count, SEQ, D)
    v_all = value_vectors.reshape(user_count, SEQ, D)
    tables = pattern.reshape(user_count, GROUP, TOK_DEV // BLOCK, FAR)
    length_all = lengths.reshape(user_count)
    band_all = widths.reshape(user_count)

    def per_user(items):
        return history_grads(items[0], items[1], items[2], items[3], items[4], items[5], items[6], relative_bucket_bias)

    grad_q, key_gradient, value_gradient, grad_b = lax.map(per_user, (q_all, g_all, k_all, v_all, tables, length_all, band_all))
    return (grad_q.reshape(N_DP, N_CTX * TOK_DEV, D), key_gradient.reshape(N_DP, N_CTX * TOK_DEV, D),
            value_gradient.reshape(N_DP, N_CTX * TOK_DEV, D), jnp.sum(grad_b, axis=0))
```

```python
import functools

import jax
import jax.numpy as jnp
from jax import lax
from jax.experimental import pallas as pl
from jax.experimental.pallas import tpu as pltpu
from jax.sharding import PartitionSpec as P

BLOCK = 128
GROUP = 8
NBUCK = 7
SEQ = 2048
F32 = jnp.float32
BF16 = jnp.bfloat16
MESH = pl.DeviceIdType.MESH


def dot(a, b, dims):
    return lax.dot_general(a, b, (dims, ((), ())), preferred_element_type=F32)


def tile(q, g, k, v, bias, scaling, keep=None):
    score = dot(k, q, ((1,), (1,))) * scaling + bias
    gate = jax.nn.sigmoid(score)
    prob = score * gate
    ds = dot(v, g, ((1,), (1,))) * (gate + prob * (1.0 - gate))
    if keep is not None:
        prob = jnp.where(keep, prob, 0.0)
        ds = jnp.where(keep, ds, 0.0)
    prob_bf = prob.astype(BF16)
    ds_bf = ds.astype(BF16)
    grad_v = dot(prob_bf, g, ((1,), (0,)))
    grad_k = dot(ds_bf, q, ((1,), (0,)))
    grad_q = dot(ds_bf, k, ((0,), (0,)))
    return grad_q, grad_k, grad_v, ds


def kernel(
    n_dp, n_ctx, heads, tokens, scaling,
    len_ref, wid_ref, pat_ref, bias_ref, q_ref, k_ref, v_ref, g_ref,
    gq_ref, gk_ref, gv_ref, gb_ref,
    kh, vh, x0, x1, x2, x4, pt0, pt2, pt4, d1, d2, d4, r1, r2, r4, aq, ak, av, ab,
    bt, bc, bd, tsq,
    sa, ra, sb, rb, sc, rc, sp2, rp2, sp4, rp4, sd1, rd1, sd2, rd2, sd4, rd4,
    sbc, rbc, sbd, rbd,
):
    me = lax.axis_index("ctx")
    row = lax.axis_index("dp")
    span = lax.rem(me, GROUP)
    even = lax.rem(me, 2) == 0
    blocks = tokens // BLOCK
    last = GROUP - 1

    def at(shift):
        return (row, me + shift)

    def send(src, dst, s, r, where):
        return pltpu.make_async_remote_copy(
            src_ref=src, dst_ref=dst, send_sem=s, recv_sem=r,
            device_id=where, device_id_type=MESH,
        )

    barrier = pltpu.get_barrier_semaphore()

    @pl.loop(1, n_ctx)
    def _(j):
        pl.semaphore_signal(
            barrier, inc=1, device_id=(row, lax.rem(me + j, n_ctx)), device_id_type=MESH
        )

    @pl.loop(1, n_dp)
    def _(j):
        pl.semaphore_signal(
            barrier, inc=1, device_id=(lax.rem(row + j, n_dp), me), device_id_type=MESH
        )

    slot = me // GROUP
    length = len_ref[0, slot]
    wide = (wid_ref[0, slot] >= 2).astype(F32)
    places = span * tokens + lax.broadcasted_iota(jnp.int32, (tokens, 1), 0)
    real = (places < length).astype(F32)
    real_bf = real.astype(BF16)
    for h in range(heads):
        c = slice(h * BLOCK, (h + 1) * BLOCK)
        x0[h, 0] = q_ref[0, :, c]
        x0[h, 1] = g_ref[0, :, c] * real_bf
    for b in range(blocks):
        for j in range(2):
            pt0[b * 2 + j : b * 2 + j + 1, :] = jnp.full((1, BLOCK), pat_ref[0, b, j].astype(F32))

    pl.semaphore_wait(barrier, n_ctx - 1 + n_dp - 1)

    def copy_a(h):
        return send(x0.at[h], x2.at[h], sa.at[h], ra.at[h], at(-2))

    def copy_b(h):
        return send(x2.at[h], x4.at[h], sb.at[h], rb.at[h], at(-2))

    def copy_c_odd(h):
        return send(x0.at[h], x1.at[h], sc.at[h], rc.at[h], at(-1))

    def copy_c_even(h):
        return send(x2.at[h], x1.at[h], sc.at[h], rc.at[h], at(1))

    def copy_p2():
        return send(pt0, pt2, sp2, rp2, at(-2))

    def copy_p4():
        return send(pt0, pt4, sp4, rp4, at(-4))

    def copy_d(h, d):
        src, dst, s, r = {1: (d1, r1, sd1, rd1), 2: (d2, r2, sd2, rd2), 4: (d4, r4, sd4, rd4)}[d]
        return send(src.at[h], dst.at[h], s.at[h], r.at[h], at(d))

    to2 = span >= 2
    to4 = span >= 4
    from1 = span + 1 <= last
    from2 = span + 2 <= last
    from4 = span + 4 <= last
    relay4 = to2 & from2
    odd_near = jnp.logical_not(even)
    even_near = even & from2

    @pl.when(to2)
    def _():
        copy_p2().start()

        @pl.loop(0, heads)
        def _(h):
            copy_a(h).start()

    @pl.when(to4)
    def _():
        copy_p4().start()

    @pl.when(odd_near)
    def _():
        @pl.loop(0, heads)
        def _(h):
            copy_c_odd(h).start()

    for h in range(heads):
        c = slice(h * BLOCK, (h + 1) * BLOCK)
        kh[h] = k_ref[0, :, c]
        vh[h] = v_ref[0, :, c] * real_bf
    ab[...] = jnp.zeros_like(ab)

    kpos = lax.broadcasted_iota(jnp.int32, (tokens, tokens), 0)
    qpos = lax.broadcasted_iota(jnp.int32, (tokens, tokens), 1)
    kb = kpos // BLOCK
    qb = qpos // BLOCK

    def colsum(x):
        return jnp.sum(x, axis=0, keepdims=True)

    def add_bias(h, bucket, value):
        ab[h, bucket : bucket + 1, :] += value

    @pl.loop(0, heads)
    def _(h):
        bias = jnp.where(qb > kb, bias_ref[h, 1], bias_ref[h, 0])
        gq, gk, gv, ds = tile(
            x0[h, 0], x0[h, 1], kh[h], vh[h], bias, scaling, kpos <= qpos
        )
        aq[h] = gq
        ak[h] = gk
        av[h] = gv
        add_bias(h, 0, colsum(ds[:BLOCK, :BLOCK]) + colsum(ds[BLOCK:, BLOCK:]))
        add_bias(h, 1, colsum(ds[:BLOCK, BLOCK:]))

    out_scale = scaling / SEQ

    def far(h, x, pt, d, level, dst):
        for b in range(blocks):
            rows = slice(b * BLOCK, (b + 1) * BLOCK)
            c1 = pt[b * 2 + level : b * 2 + level + 1, :]
            c0 = 1.0 - c1
            k = (kh[h, :BLOCK, :] * c0 + kh[h, BLOCK:, :] * c1).astype(BF16)
            v = (vh[h, :BLOCK, :] * c0 + vh[h, BLOCK:, :] * c1).astype(BF16)
            u0 = min(blocks * d + b, NBUCK - 1)
            u1 = min(blocks * d + b - 1, NBUCK - 1)
            bias = c0 * bias_ref[h, u0] + c1 * bias_ref[h, u1]
            gq, gk, gv, ds = tile(x[h, 0, rows, :], x[h, 1, rows, :], k, v, bias, scaling)
            dst[h, rows, :] = (gq * out_scale).astype(BF16)
            ak[h, :BLOCK, :] += gk * c0
            ak[h, BLOCK:, :] += gk * c1
            av[h, :BLOCK, :] += gv * c0
            av[h, BLOCK:, :] += gv * c1
            total = colsum(ds)
            if u0 == u1:
                add_bias(h, u0, total)
            else:
                add_bias(h, u0, total * c0)
                add_bias(h, u1, total * c1)

    @pl.when(from2)
    def _():
        copy_p2().wait_recv()

    @pl.loop(0, heads)
    def _(h):
        @pl.when(from2)
        def _():
            copy_a(h).wait_recv()

            @pl.when(to2)
            def _():
                copy_b(h).start()

            @pl.when(even)
            def _():
                copy_c_even(h).start()

            far(h, x2, pt2, 2, 0, d2)
            copy_d(h, 2).start()

        @pl.when(from1)
        def _():
            copy_c_odd(h).wait_recv()
            bias = jnp.where(qb + 1 == kb, bias_ref[h, 1], bias_ref[h, 2])
            weight = jnp.where(qb + 1 == kb, 1.0, jnp.where(qb == kb, wide, 0.0))
            gq, gk, gv, ds = tile(
                x1[h, 0], x1[h, 1], kh[h], vh[h], bias, scaling, weight > 0.0
            )
            d1[h] = (gq * out_scale).astype(BF16)
            copy_d(h, 1).start()
            ak[h] += gk
            av[h] += gv
            add_bias(h, 1, colsum(ds[BLOCK:, :BLOCK]))
            add_bias(h, 2, colsum(ds[:BLOCK, :BLOCK]) + colsum(ds[BLOCK:, BLOCK:]))

    @pl.when(from4)
    def _():
        copy_p4().wait_recv()

        @pl.loop(0, heads)
        def _(h):
            copy_b(h).wait_recv()
            far(h, x4, pt4, 4, 1, d4)
            copy_d(h, 4).start()

    lane = lax.broadcasted_iota(jnp.int32, (8, BLOCK), 1)
    mine = jnp.zeros((8, BLOCK), F32)
    for h in range(heads):
        mine += jnp.where(lane == h, jnp.sum(ab[h], axis=1, keepdims=True), 0.0)
    bt[0] = mine * (1.0 / SEQ)

    def copy_bc(j, source):
        peer = lax.rem(me + j, n_ctx)
        return send(bt.at[0], bc.at[source], sbc.at[j], rbc.at[source], (row, peer))

    def copy_bd(j, source):
        peer = lax.rem(row + j, n_dp)
        return send(bt.at[1], bd.at[source], sbd.at[j], rbd.at[source], (peer, me))

    @pl.loop(1, n_ctx)
    def _(j):
        copy_bc(j, me).start()

    for h in range(heads):
        c = slice(h * BLOCK, (h + 1) * BLOCK)
        gk_ref[0, :, c] = (ak[h] * out_scale).astype(BF16)
        gv_ref[0, :, c] = (av[h] * (real * (1.0 / SEQ))).astype(BF16)

    bc[me] = bt[0]

    @pl.loop(1, n_ctx)
    def _(j):
        copy_bc(j, lax.rem(me + j, n_ctx)).wait_recv()

    bt[1] = jnp.sum(bc[...], axis=0)

    @pl.loop(1, n_dp)
    def _(j):
        copy_bd(j, row).start()

    @pl.loop(0, heads)
    def _(h):
        aq[h] = aq[h] * out_scale

        @pl.when(span >= 1)
        def _():
            copy_d(h, 1).wait_recv()
            aq[h] += r1[h].astype(F32)

        @pl.when(span >= 2)
        def _():
            copy_d(h, 2).wait_recv()
            aq[h] += r2[h].astype(F32)

        @pl.when(span >= 4)
        def _():
            copy_d(h, 4).wait_recv()
            aq[h] += r4[h].astype(F32)

    for h in range(heads):
        gq_ref[0, :, h * BLOCK : (h + 1) * BLOCK] = aq[h].astype(BF16)

    bd[row] = bt[1]

    @pl.loop(1, n_dp)
    def _(j):
        copy_bd(j, lax.rem(row + j, n_dp)).wait_recv()

    tsq[...] = jnp.zeros_like(tsq)
    tsq[:8, :] = jnp.sum(bd[...], axis=0)
    gb_ref[...] = tsq[...].T[:heads, :NBUCK]

    @pl.when(to2)
    def _():
        copy_p2().wait_send()

        @pl.loop(0, heads)
        def _(h):
            copy_a(h).wait_send()

    @pl.when(to4)
    def _():
        copy_p4().wait_send()

    @pl.when(relay4)
    def _():
        @pl.loop(0, heads)
        def _(h):
            copy_b(h).wait_send()

    @pl.when(odd_near | even_near)
    def _():
        @pl.loop(0, heads)
        def _(h):
            copy_c_odd(h).wait_send()

    for d, there in ((1, from1), (2, from2), (4, from4)):
        @pl.when(there)
        def _(d=d):
            @pl.loop(0, heads)
            def _(h):
                copy_d(h, d).wait_send()

    @pl.loop(1, n_ctx)
    def _(j):
        copy_bc(j, me).wait_send()

    @pl.loop(1, n_dp)
    def _(j):
        copy_bd(j, row).wait_send()


def on_device(
    queries, key_vectors, value_vectors, grad_output, pattern, lengths, widths, relative_bucket_bias,
    n_dp, n_ctx,
):
    tokens, width = queries.shape[1:]
    heads = relative_bucket_bias.shape[0]
    dim = width // heads
    vm = pl.BlockSpec(memory_space=pltpu.VMEM)
    sm = pl.BlockSpec(memory_space=pltpu.SMEM)
    dma = pltpu.SemaphoreType.DMA
    x = pltpu.VMEM((heads, 2, tokens, dim), BF16)
    half = pltpu.VMEM((heads, tokens, dim), BF16)
    acc = pltpu.VMEM((heads, tokens, dim), F32)
    pat = pltpu.VMEM((8, BLOCK), F32)
    per_head = dma((heads,))
    rows = jax.ShapeDtypeStruct(queries.shape, BF16)
    return pl.pallas_call(
        functools.partial(kernel, n_dp, n_ctx, heads, tokens, dim ** (-0.5)),
        out_shape=(rows, rows, rows, jax.ShapeDtypeStruct(relative_bucket_bias.shape, F32)),
        in_specs=[sm] * 4 + [vm] * 4,
        out_specs=(vm,) * 4,
        scratch_shapes=[half, half, x, x, x, x, pat, pat, pat]
        + [half] * 6
        + [acc] * 3
        + [
            pltpu.VMEM((heads, 8, BLOCK), F32),
            pltpu.VMEM((2, 8, BLOCK), F32),
            pltpu.VMEM((n_ctx, 8, BLOCK), F32),
            pltpu.VMEM((n_dp, 8, BLOCK), F32),
            pltpu.VMEM((BLOCK, BLOCK), F32),
        ]
        + [per_head] * 6
        + [dma, dma, dma, dma]
        + [per_head] * 6
        + [dma((n_ctx,)), dma((n_ctx,)), dma((n_dp,)), dma((n_dp,))],
        compiler_params=pltpu.CompilerParams(
            collective_id=0, has_side_effects=True, vmem_limit_bytes=40 * 2**20
        ),
    )(lengths, widths, pattern, relative_bucket_bias, queries, key_vectors, value_vectors, grad_output)


def solution(mesh):
    split = P("dp", "ctx", None)
    in_specs = (split,) * 5 + (P("dp", None), P("dp", None), P())
    body = functools.partial(on_device, n_dp=mesh.shape["dp"], n_ctx=mesh.shape["ctx"])
    return jax.shard_map(
        body, mesh=mesh, in_specs=in_specs, out_specs=(split,) * 3 + (P(),), check_vma=False
    )
```

```python
import functools

import jax
import jax.numpy as jnp
from jax import lax
from jax.experimental import pallas as pl
from jax.experimental.pallas import tpu as pltpu
from jax.sharding import PartitionSpec as P

BLOCK = 128
GROUP = 8
NBUCK = 7
SEQ = 2048
F32 = jnp.float32
BF16 = jnp.bfloat16
VMEM_LIMIT = 63 * 2**20
MESH = pl.DeviceIdType.MESH


def dot(a, b, dims):
    return lax.dot_general(a, b, (dims, ((), ())), preferred_element_type=F32)


def tile(q, g, k, v, bias, scaling, keep=None):
    score = dot(k, q, ((1,), (1,))) * scaling + bias
    gate = jax.nn.sigmoid(score)
    prob = score * gate
    ds = dot(v, g, ((1,), (1,))) * (gate + prob * (1.0 - gate))
    if keep is not None:
        prob = jnp.where(keep, prob, 0.0)
        ds = jnp.where(keep, ds, 0.0)
    prob_bf = prob.astype(BF16)
    ds_bf = ds.astype(BF16)
    grad_v = dot(prob_bf, g, ((1,), (0,)))
    grad_k = dot(ds_bf, q, ((1,), (0,)))
    grad_q = dot(ds_bf, k, ((0,), (0,)))
    return grad_q, grad_k, grad_v, ds


def kernel(
    n_dp, n_ctx, heads, tokens, scaling,
    len_in, wid_in, pat_in, bias_in, q_ref, k_ref, v_ref, g_ref,
    gq_ref, gk_ref, gv_ref, gb_ref,
    len_ref, wid_ref, pat_ref, bias_ref, sem_small, sem_q, sem_g, sem_k, sem_v,
    kh, vh, x0, x1, x2, x4, pt0, pt2, pt4, d1, d2, d4, r1, r2, r4, aq, ak, av, ab,
    bt, bc, bd, tsq,
    sa, ra, sb, rb, sc, rc, sp2, rp2, sp4, rp4, sd1, rd1, sd2, rd2, sd4, rd4,
    sbc, rbc, sbd, rbd,
):
    me = lax.axis_index("ctx")
    row = lax.axis_index("dp")
    span = lax.rem(me, GROUP)
    even = lax.rem(me, 2) == 0
    blocks = tokens // BLOCK
    last = GROUP - 1

    def at(shift):
        return (row, me + shift)

    def send(src, dst, s, r, where):
        return pltpu.make_async_remote_copy(
            src_ref=src, dst_ref=dst, send_sem=s, recv_sem=r,
            device_id=where, device_id_type=MESH,
        )

    small = [
        pltpu.make_async_copy(src, dst, sem_small.at[i])
        for i, (src, dst) in enumerate(
            ((len_in, len_ref), (wid_in, wid_ref), (pat_in, pat_ref), (bias_in, bias_ref))
        )
    ]
    for copy in small:
        copy.start()

    def fetch(src, dst, sem):
        copies = [
            pltpu.make_async_copy(src.at[0, :, pl.ds(h * BLOCK, BLOCK)], dst(h), sem.at[h])
            for h in range(heads)
        ]
        for copy in copies:
            copy.start()
        return copies

    fetch_g = fetch(g_ref, lambda h: x0.at[h, 1], sem_g)
    fetch_q = fetch(q_ref, lambda h: x0.at[h, 0], sem_q)
    fetch_k = fetch(k_ref, lambda h: kh.at[h], sem_k)
    fetch_v = fetch(v_ref, lambda h: vh.at[h], sem_v)

    barrier = pltpu.get_barrier_semaphore()

    @pl.loop(1, n_ctx)
    def _(j):
        pl.semaphore_signal(
            barrier, inc=1, device_id=(row, lax.rem(me + j, n_ctx)), device_id_type=MESH
        )

    @pl.loop(1, n_dp)
    def _(j):
        pl.semaphore_signal(
            barrier, inc=1, device_id=(lax.rem(row + j, n_dp), me), device_id_type=MESH
        )

    for copy in small:
        copy.wait()
    slot = me // GROUP
    length = len_ref[0, slot]
    wide = (wid_ref[0, slot] >= 2).astype(F32)
    places = span * tokens + lax.broadcasted_iota(jnp.int32, (tokens, 1), 0)
    real = (places < length).astype(F32)
    real_bf = real.astype(BF16)
    for h in range(heads):
        fetch_g[h].wait()
        x0[h, 1] = x0[h, 1] * real_bf
    for b in range(blocks):
        for j in range(2):
            pt0[b * 2 + j : b * 2 + j + 1, :] = jnp.full((1, BLOCK), pat_ref[0, b, j].astype(F32))

    for h in range(heads):
        fetch_q[h].wait()
    pl.semaphore_wait(barrier, n_ctx - 1 + n_dp - 1)

    def copy_a(h):
        return send(x0.at[h], x2.at[h], sa.at[h], ra.at[h], at(-2))

    def copy_b(h):
        return send(x2.at[h], x4.at[h], sb.at[h], rb.at[h], at(-2))

    def copy_c_odd(h):
        return send(x0.at[h], x1.at[h], sc.at[h], rc.at[h], at(-1))

    def copy_c_even(h):
        return send(x2.at[h], x1.at[h], sc.at[h], rc.at[h], at(1))

    def copy_p2():
        return send(pt0, pt2, sp2, rp2, at(-2))

    def copy_p4():
        return send(pt0, pt4, sp4, rp4, at(-4))

    def copy_d(h, d):
        src, dst, s, r = {1: (d1, r1, sd1, rd1), 2: (d2, r2, sd2, rd2), 4: (d4, r4, sd4, rd4)}[d]
        return send(src.at[h], dst.at[h], s.at[h], r.at[h], at(d))

    to2 = span >= 2
    to4 = span >= 4
    from1 = span + 1 <= last
    from2 = span + 2 <= last
    from4 = span + 4 <= last
    relay4 = to2 & from2
    odd_near = jnp.logical_not(even)
    even_near = even & from2

    @pl.when(to2)
    def _():
        copy_p2().start()

        @pl.loop(0, heads)
        def _(h):
            copy_a(h).start()

    @pl.when(to4)
    def _():
        copy_p4().start()

    @pl.when(odd_near)
    def _():
        @pl.loop(0, heads)
        def _(h):
            copy_c_odd(h).start()

    for h in range(heads):
        fetch_k[h].wait()
        fetch_v[h].wait()
        vh[h] = vh[h] * real_bf
    ab[...] = jnp.zeros_like(ab)

    kpos = lax.broadcasted_iota(jnp.int32, (tokens, tokens), 0)
    qpos = lax.broadcasted_iota(jnp.int32, (tokens, tokens), 1)
    kb = kpos // BLOCK
    qb = qpos // BLOCK

    def colsum(x):
        return jnp.sum(x, axis=0, keepdims=True)

    def add_bias(h, bucket, value):
        ab[h, bucket : bucket + 1, :] += value

    @pl.loop(0, heads)
    def _(h):
        bias = jnp.where(qb > kb, bias_ref[h, 1], bias_ref[h, 0])
        gq, gk, gv, ds = tile(
            x0[h, 0], x0[h, 1], kh[h], vh[h], bias, scaling, kpos <= qpos
        )
        aq[h] = gq
        ak[h] = gk
        av[h] = gv
        add_bias(h, 0, colsum(ds[:BLOCK, :BLOCK]) + colsum(ds[BLOCK:, BLOCK:]))
        add_bias(h, 1, colsum(ds[:BLOCK, BLOCK:]))

        @pl.when(from2)
        def _():
            copy_a(h).wait_recv()

            @pl.when(to2)
            def _():
                copy_b(h).start()

            @pl.when(even)
            def _():
                copy_c_even(h).start()

    out_scale = scaling / SEQ

    def far(h, x, pt, d, level, dst):
        for b in range(blocks):
            rows = slice(b * BLOCK, (b + 1) * BLOCK)
            c1 = pt[b * 2 + level : b * 2 + level + 1, :]
            c0 = 1.0 - c1
            k = (kh[h, :BLOCK, :] * c0 + kh[h, BLOCK:, :] * c1).astype(BF16)
            v = (vh[h, :BLOCK, :] * c0 + vh[h, BLOCK:, :] * c1).astype(BF16)
            u0 = min(blocks * d + b, NBUCK - 1)
            u1 = min(blocks * d + b - 1, NBUCK - 1)
            bias = c0 * bias_ref[h, u0] + c1 * bias_ref[h, u1]
            gq, gk, gv, ds = tile(x[h, 0, rows, :], x[h, 1, rows, :], k, v, bias, scaling)
            dst[h, rows, :] = (gq * out_scale).astype(BF16)
            ak[h, :BLOCK, :] += gk * c0
            ak[h, BLOCK:, :] += gk * c1
            av[h, :BLOCK, :] += gv * c0
            av[h, BLOCK:, :] += gv * c1
            total = colsum(ds)
            if u0 == u1:
                add_bias(h, u0, total)
            else:
                add_bias(h, u0, total * c0)
                add_bias(h, u1, total * c1)

    @pl.when(from2)
    def _():
        copy_p2().wait_recv()

    @pl.loop(0, heads)
    def _(h):
        @pl.when(from2)
        def _():
            far(h, x2, pt2, 2, 0, d2)
            copy_d(h, 2).start()

        @pl.when(from1)
        def _():
            copy_c_odd(h).wait_recv()
            bias = jnp.where(qb + 1 == kb, bias_ref[h, 1], bias_ref[h, 2])
            weight = jnp.where(qb + 1 == kb, 1.0, jnp.where(qb == kb, wide, 0.0))
            gq, gk, gv, ds = tile(
                x1[h, 0], x1[h, 1], kh[h], vh[h], bias, scaling, weight > 0.0
            )
            d1[h] = (gq * out_scale).astype(BF16)
            copy_d(h, 1).start()
            ak[h] += gk
            av[h] += gv
            add_bias(h, 1, colsum(ds[BLOCK:, :BLOCK]))
            add_bias(h, 2, colsum(ds[:BLOCK, :BLOCK]) + colsum(ds[BLOCK:, BLOCK:]))

    @pl.when(from4)
    def _():
        copy_p4().wait_recv()

        @pl.loop(0, heads)
        def _(h):
            copy_b(h).wait_recv()
            far(h, x4, pt4, 4, 1, d4)
            copy_d(h, 4).start()

    lane = lax.broadcasted_iota(jnp.int32, (8, BLOCK), 1)
    mine = jnp.zeros((8, BLOCK), F32)
    for h in range(heads):
        mine += jnp.where(lane == h, jnp.sum(ab[h], axis=1, keepdims=True), 0.0)
    bt[0] = mine * (1.0 / SEQ)

    def copy_bc(j, source):
        peer = lax.rem(me + j, n_ctx)
        return send(bt.at[0], bc.at[source], sbc.at[j], rbc.at[source], (row, peer))

    def copy_bd(j, source):
        peer = lax.rem(row + j, n_dp)
        return send(bt.at[1], bd.at[source], sbd.at[j], rbd.at[source], (peer, me))

    @pl.loop(1, n_ctx)
    def _(j):
        copy_bc(j, me).start()

    for h in range(heads):
        c = slice(h * BLOCK, (h + 1) * BLOCK)
        gk_ref[0, :, c] = (ak[h] * out_scale).astype(BF16)
        gv_ref[0, :, c] = (av[h] * (real * (1.0 / SEQ))).astype(BF16)

    bc[me] = bt[0]

    @pl.loop(1, n_ctx)
    def _(j):
        copy_bc(j, lax.rem(me + j, n_ctx)).wait_recv()

    bt[1] = jnp.sum(bc[...], axis=0)

    @pl.loop(1, n_dp)
    def _(j):
        copy_bd(j, row).start()

    @pl.loop(0, heads)
    def _(h):
        aq[h] = aq[h] * out_scale

        @pl.when(span >= 1)
        def _():
            copy_d(h, 1).wait_recv()
            aq[h] += r1[h].astype(F32)

        @pl.when(span >= 2)
        def _():
            copy_d(h, 2).wait_recv()
            aq[h] += r2[h].astype(F32)

        @pl.when(span >= 4)
        def _():
            copy_d(h, 4).wait_recv()
            aq[h] += r4[h].astype(F32)

    for h in range(heads):
        gq_ref[0, :, h * BLOCK : (h + 1) * BLOCK] = aq[h].astype(BF16)

    bd[row] = bt[1]

    @pl.loop(1, n_dp)
    def _(j):
        copy_bd(j, lax.rem(row + j, n_dp)).wait_recv()

    tsq[...] = jnp.zeros_like(tsq)
    tsq[:8, :] = jnp.sum(bd[...], axis=0)
    gb_ref[...] = tsq[...].T[:heads, :NBUCK]

    @pl.when(to2)
    def _():
        copy_p2().wait_send()

        @pl.loop(0, heads)
        def _(h):
            copy_a(h).wait_send()

    @pl.when(to4)
    def _():
        copy_p4().wait_send()

    @pl.when(relay4)
    def _():
        @pl.loop(0, heads)
        def _(h):
            copy_b(h).wait_send()

    @pl.when(odd_near | even_near)
    def _():
        @pl.loop(0, heads)
        def _(h):
            copy_c_odd(h).wait_send()

    for d, there in ((1, from1), (2, from2), (4, from4)):
        @pl.when(there)
        def _(d=d):
            @pl.loop(0, heads)
            def _(h):
                copy_d(h, d).wait_send()

    @pl.loop(1, n_ctx)
    def _(j):
        copy_bc(j, me).wait_send()

    @pl.loop(1, n_dp)
    def _(j):
        copy_bd(j, row).wait_send()


def copy_kernel(*refs):
    *refs, sems = refs
    half = len(refs) // 2
    copies = [
        pltpu.make_async_copy(refs[i], refs[half + i], sems.at[i]) for i in range(half)
    ]
    for copy in copies:
        copy.start()
    for copy in copies:
        copy.wait()


def copy_out(arrays):
    any_ = pl.BlockSpec(memory_space=pl.ANY)
    n = len(arrays)
    return pl.pallas_call(
        copy_kernel,
        out_shape=tuple(jax.ShapeDtypeStruct(a.shape, a.dtype) for a in arrays),
        in_specs=[any_] * n,
        out_specs=(any_,) * n,
        scratch_shapes=[pltpu.SemaphoreType.DMA((n,))],
    )(*arrays)


def on_device(
    queries, key_vectors, value_vectors, grad_output, pattern, lengths, widths, relative_bucket_bias,
    n_dp, n_ctx,
):
    tokens, width = queries.shape[1:]
    heads = relative_bucket_bias.shape[0]
    dim = width // heads
    vm = pl.BlockSpec(memory_space=pltpu.VMEM)
    hbm = pl.BlockSpec(memory_space=pl.ANY)
    dma = pltpu.SemaphoreType.DMA
    x = pltpu.VMEM((heads, 2, tokens, dim), BF16)
    half = pltpu.VMEM((heads, tokens, dim), BF16)
    acc = pltpu.VMEM((heads, tokens, dim), F32)
    pat = pltpu.VMEM((8, BLOCK), F32)
    per_head = dma((heads,))
    rows = jax.ShapeDtypeStruct(queries.shape, BF16)
    small = (lengths, widths, pattern, relative_bucket_bias)
    results = pl.pallas_call(
        functools.partial(kernel, n_dp, n_ctx, heads, tokens, dim ** (-0.5)),
        out_shape=(rows, rows, rows, jax.ShapeDtypeStruct(relative_bucket_bias.shape, F32)),
        in_specs=[hbm] * 8,
        out_specs=(vm,) * 4,
        scratch_shapes=[pltpu.SMEM(a.shape, a.dtype) for a in small]
        + [dma((len(small),))]
        + [per_head] * 4
        + [half, half, x, x, x, x, pat, pat, pat]
        + [half] * 6
        + [acc] * 3
        + [
            pltpu.VMEM((heads, 8, BLOCK), F32),
            pltpu.VMEM((2, 8, BLOCK), F32),
            pltpu.VMEM((n_ctx, 8, BLOCK), F32),
            pltpu.VMEM((n_dp, 8, BLOCK), F32),
            pltpu.VMEM((BLOCK, BLOCK), F32),
        ]
        + [per_head] * 6
        + [dma, dma, dma, dma]
        + [per_head] * 6
        + [dma((n_ctx,)), dma((n_ctx,)), dma((n_dp,)), dma((n_dp,))],
        compiler_params=pltpu.CompilerParams(
            collective_id=0, has_side_effects=True, vmem_limit_bytes=VMEM_LIMIT
        ),
    )(*small, queries, key_vectors, value_vectors, grad_output)
    return copy_out(results)


def solution(mesh):
    split = P("dp", "ctx", None)
    in_specs = (split,) * 5 + (P("dp", None), P("dp", None), P())
    body = functools.partial(on_device, n_dp=mesh.shape["dp"], n_ctx=mesh.shape["ctx"])
    return jax.shard_map(
        body, mesh=mesh, in_specs=in_specs, out_specs=(split,) * 3 + (P(),), check_vma=False
    )
```

```python
import functools

import jax
import jax.numpy as jnp
from jax import lax
from jax.experimental import pallas as pl
from jax.experimental.pallas import tpu as pltpu
from jax.sharding import PartitionSpec as P

BLOCK = 128
GROUP = 8
NBUCK = 7
SEQ = 2048
F32 = jnp.float32
BF16 = jnp.bfloat16
VMEM_LIMIT = 63 * 2**20
MESH = pl.DeviceIdType.MESH


def dot(a, b, dims):
    return lax.dot_general(a, b, (dims, ((), ())), preferred_element_type=F32)


def tile(q, g, k, v, bias, scaling, keep=None):
    score = dot(k, q, ((1,), (1,))) * scaling + bias
    gate = jax.nn.sigmoid(score)
    prob = score * gate
    ds = dot(v, g, ((1,), (1,))) * (gate + prob * (1.0 - gate))
    if keep is not None:
        prob = jnp.where(keep, prob, 0.0)
        ds = jnp.where(keep, ds, 0.0)
    prob_bf = prob.astype(BF16)
    ds_bf = ds.astype(BF16)
    grad_v = dot(prob_bf, g, ((1,), (0,)))
    grad_k = dot(ds_bf, q, ((1,), (0,)))
    grad_q = dot(ds_bf, k, ((0,), (0,)))
    return grad_q, grad_k, grad_v, ds


def kernel(
    n_dp, n_ctx, heads, tokens, scaling,
    len_in, wid_in, pat_in, bias_in, q_ref, k_ref, v_ref, g_ref,
    gq_ref, gk_ref, gv_ref, gb_ref,
    len_ref, wid_ref, pat_ref, bias_ref, sem_small, sem_q, sem_g, sem_k, sem_v,
    kh, vh, x0, x1, x2, x4, pt0, pt2, pt4, d1, d2, d4, r1, r2, r4, aq, ak, av, ab,
    bt, bc, bd, tsq,
    sa, ra, sb, rb, sc, rc, sp2, rp2, sp4, rp4, sd1, rd1, sd2, rd2, sd4, rd4,
    sbc, rbc, sbd, rbd,
):
    me = lax.axis_index("ctx")
    row = lax.axis_index("dp")
    span = lax.rem(me, GROUP)
    even = lax.rem(me, 2) == 0
    blocks = tokens // BLOCK
    last = GROUP - 1

    def at(shift):
        return (row, me + shift)

    def send(src, dst, s, r, where):
        return pltpu.make_async_remote_copy(
            src_ref=src, dst_ref=dst, send_sem=s, recv_sem=r,
            device_id=where, device_id_type=MESH,
        )

    small = [
        pltpu.make_async_copy(src, dst, sem_small.at[i])
        for i, (src, dst) in enumerate(
            ((len_in, len_ref), (wid_in, wid_ref), (pat_in, pat_ref), (bias_in, bias_ref))
        )
    ]
    for copy in small:
        copy.start()

    def fetch(src, dst, sem):
        copies = [
            pltpu.make_async_copy(src.at[0, :, pl.ds(h * BLOCK, BLOCK)], dst(h), sem.at[h])
            for h in range(heads)
        ]
        for copy in copies:
            copy.start()
        return copies

    fetch_g = fetch(g_ref, lambda h: x0.at[h, 1], sem_g)
    fetch_q = fetch(q_ref, lambda h: x0.at[h, 0], sem_q)
    fetch_k = fetch(k_ref, lambda h: kh.at[h], sem_k)
    fetch_v = fetch(v_ref, lambda h: vh.at[h], sem_v)

    barrier = pltpu.get_barrier_semaphore()

    @pl.loop(1, n_ctx)
    def _(j):
        pl.semaphore_signal(
            barrier, inc=1, device_id=(row, lax.rem(me + j, n_ctx)), device_id_type=MESH
        )

    @pl.loop(1, n_dp)
    def _(j):
        pl.semaphore_signal(
            barrier, inc=1, device_id=(lax.rem(row + j, n_dp), me), device_id_type=MESH
        )

    for copy in small:
        copy.wait()
    slot = me // GROUP
    length = len_ref[0, slot]
    wide = (wid_ref[0, slot] >= 2).astype(F32)
    places = span * tokens + lax.broadcasted_iota(jnp.int32, (tokens, 1), 0)
    real = (places < length).astype(F32)
    real_bf = real.astype(BF16)
    for h in range(heads):
        fetch_g[h].wait()
        x0[h, 1] = x0[h, 1] * real_bf
    for b in range(blocks):
        for j in range(2):
            pt0[b * 2 + j : b * 2 + j + 1, :] = jnp.full((1, BLOCK), pat_ref[0, b, j].astype(F32))

    for h in range(heads):
        fetch_q[h].wait()
    pl.semaphore_wait(barrier, n_ctx - 1 + n_dp - 1)

    def copy_a(h):
        return send(x0.at[h], x2.at[h], sa.at[h], ra.at[h], at(-2))

    def copy_b(h):
        return send(x2.at[h], x4.at[h], sb.at[h], rb.at[h], at(-2))

    def copy_c_odd(h):
        return send(x0.at[h], x1.at[h], sc.at[h], rc.at[h], at(-1))

    def copy_c_even(h):
        return send(x2.at[h], x1.at[h], sc.at[h], rc.at[h], at(1))

    def copy_p2():
        return send(pt0, pt2, sp2, rp2, at(-2))

    def copy_p4():
        return send(pt0, pt4, sp4, rp4, at(-4))

    def copy_d(h, d):
        src, dst, s, r = {1: (d1, r1, sd1, rd1), 2: (d2, r2, sd2, rd2), 4: (d4, r4, sd4, rd4)}[d]
        return send(src.at[h], dst.at[h], s.at[h], r.at[h], at(d))

    to2 = span >= 2
    to4 = span >= 4
    from1 = span + 1 <= last
    from2 = span + 2 <= last
    from4 = span + 4 <= last
    relay4 = to2 & from2
    odd_near = jnp.logical_not(even)
    even_near = even & from2

    @pl.when(to2)
    def _():
        copy_p2().start()

        @pl.loop(0, heads)
        def _(h):
            copy_a(h).start()

    @pl.when(to4)
    def _():
        copy_p4().start()

    @pl.when(odd_near)
    def _():
        @pl.loop(0, heads)
        def _(h):
            copy_c_odd(h).start()

    for h in range(heads):
        fetch_k[h].wait()
        fetch_v[h].wait()
        vh[h] = vh[h] * real_bf
    ab[...] = jnp.zeros_like(ab)

    kpos = lax.broadcasted_iota(jnp.int32, (tokens, tokens), 0)
    qpos = lax.broadcasted_iota(jnp.int32, (tokens, tokens), 1)
    kb = kpos // BLOCK
    qb = qpos // BLOCK

    def colsum(x):
        return jnp.sum(x, axis=0, keepdims=True)

    def add_bias(h, bucket, value):
        ab[h, bucket : bucket + 1, :] += value

    out_scale = scaling / SEQ

    def far(h, x, pt, d, level, dst):
        for b in range(blocks):
            rows = slice(b * BLOCK, (b + 1) * BLOCK)
            c1 = pt[b * 2 + level : b * 2 + level + 1, :]
            c0 = 1.0 - c1
            k = (kh[h, :BLOCK, :] * c0 + kh[h, BLOCK:, :] * c1).astype(BF16)
            v = (vh[h, :BLOCK, :] * c0 + vh[h, BLOCK:, :] * c1).astype(BF16)
            u0 = min(blocks * d + b, NBUCK - 1)
            u1 = min(blocks * d + b - 1, NBUCK - 1)
            bias = c0 * bias_ref[h, u0] + c1 * bias_ref[h, u1]
            gq, gk, gv, ds = tile(x[h, 0, rows, :], x[h, 1, rows, :], k, v, bias, scaling)
            dst[h, rows, :] = (gq * out_scale).astype(BF16)
            ak[h, :BLOCK, :] += gk * c0
            ak[h, BLOCK:, :] += gk * c1
            av[h, :BLOCK, :] += gv * c0
            av[h, BLOCK:, :] += gv * c1
            total = colsum(ds)
            if u0 == u1:
                add_bias(h, u0, total)
            else:
                add_bias(h, u0, total * c0)
                add_bias(h, u1, total * c1)

    def near(h):
        @pl.when(from1)
        def _():
            copy_c_odd(h).wait_recv()
            bias = jnp.where(qb + 1 == kb, bias_ref[h, 1], bias_ref[h, 2])
            weight = jnp.where(qb + 1 == kb, 1.0, jnp.where(qb == kb, wide, 0.0))
            gq, gk, gv, ds = tile(
                x1[h, 0], x1[h, 1], kh[h], vh[h], bias, scaling, weight > 0.0
            )
            d1[h] = (gq * out_scale).astype(BF16)
            copy_d(h, 1).start()
            ak[h] += gk
            av[h] += gv
            add_bias(h, 1, colsum(ds[BLOCK:, :BLOCK]))
            add_bias(h, 2, colsum(ds[:BLOCK, :BLOCK]) + colsum(ds[BLOCK:, BLOCK:]))

    @pl.when(from2)
    def _():
        copy_p2().wait_recv()

    @pl.loop(0, heads)
    def _(h):
        bias = jnp.where(qb > kb, bias_ref[h, 1], bias_ref[h, 0])
        gq, gk, gv, ds = tile(
            x0[h, 0], x0[h, 1], kh[h], vh[h], bias, scaling, kpos <= qpos
        )
        aq[h] = gq
        ak[h] = gk
        av[h] = gv
        add_bias(h, 0, colsum(ds[:BLOCK, :BLOCK]) + colsum(ds[BLOCK:, BLOCK:]))
        add_bias(h, 1, colsum(ds[:BLOCK, BLOCK:]))

        @pl.when(from2)
        def _():
            copy_a(h).wait_recv()

            @pl.when(to2)
            def _():
                copy_b(h).start()

            @pl.when(even)
            def _():
                copy_c_even(h).start()

            far(h, x2, pt2, 2, 0, d2)
            copy_d(h, 2).start()

        near(h)

    @pl.when(from4)
    def _():
        copy_p4().wait_recv()

        @pl.loop(0, heads)
        def _(h):
            copy_b(h).wait_recv()
            far(h, x4, pt4, 4, 1, d4)
            copy_d(h, 4).start()

    lane = lax.broadcasted_iota(jnp.int32, (8, BLOCK), 1)
    mine = jnp.zeros((8, BLOCK), F32)
    for h in range(heads):
        mine += jnp.where(lane == h, jnp.sum(ab[h], axis=1, keepdims=True), 0.0)
    bt[0] = mine * (1.0 / SEQ)

    def copy_bc(j, source):
        peer = lax.rem(me + j, n_ctx)
        return send(bt.at[0], bc.at[source], sbc.at[j], rbc.at[source], (row, peer))

    def copy_bd(j, source):
        peer = lax.rem(row + j, n_dp)
        return send(bt.at[1], bd.at[source], sbd.at[j], rbd.at[source], (peer, me))

    @pl.loop(1, n_ctx)
    def _(j):
        copy_bc(j, me).start()

    for h in range(heads):
        c = slice(h * BLOCK, (h + 1) * BLOCK)
        gk_ref[0, :, c] = (ak[h] * out_scale).astype(BF16)
        gv_ref[0, :, c] = (av[h] * (real * (1.0 / SEQ))).astype(BF16)

    bc[me] = bt[0]

    @pl.loop(1, n_ctx)
    def _(j):
        copy_bc(j, lax.rem(me + j, n_ctx)).wait_recv()

    bt[1] = jnp.sum(bc[...], axis=0)

    @pl.loop(1, n_dp)
    def _(j):
        copy_bd(j, row).start()

    @pl.loop(0, heads)
    def _(h):
        aq[h] = aq[h] * out_scale

        @pl.when(span >= 1)
        def _():
            copy_d(h, 1).wait_recv()
            aq[h] += r1[h].astype(F32)

        @pl.when(span >= 2)
        def _():
            copy_d(h, 2).wait_recv()
            aq[h] += r2[h].astype(F32)

        @pl.when(span >= 4)
        def _():
            copy_d(h, 4).wait_recv()
            aq[h] += r4[h].astype(F32)

    for h in range(heads):
        gq_ref[0, :, h * BLOCK : (h + 1) * BLOCK] = aq[h].astype(BF16)

    bd[row] = bt[1]

    @pl.loop(1, n_dp)
    def _(j):
        copy_bd(j, lax.rem(row + j, n_dp)).wait_recv()

    tsq[...] = jnp.zeros_like(tsq)
    tsq[:8, :] = jnp.sum(bd[...], axis=0)
    gb_ref[...] = tsq[...].T[:heads, :NBUCK]

    @pl.when(to2)
    def _():
        copy_p2().wait_send()

        @pl.loop(0, heads)
        def _(h):
            copy_a(h).wait_send()

    @pl.when(to4)
    def _():
        copy_p4().wait_send()

    @pl.when(relay4)
    def _():
        @pl.loop(0, heads)
        def _(h):
            copy_b(h).wait_send()

    @pl.when(odd_near | even_near)
    def _():
        @pl.loop(0, heads)
        def _(h):
            copy_c_odd(h).wait_send()

    for d, there in ((1, from1), (2, from2), (4, from4)):
        @pl.when(there)
        def _(d=d):
            @pl.loop(0, heads)
            def _(h):
                copy_d(h, d).wait_send()

    @pl.loop(1, n_ctx)
    def _(j):
        copy_bc(j, me).wait_send()

    @pl.loop(1, n_dp)
    def _(j):
        copy_bd(j, row).wait_send()


def copy_kernel(n, *refs):
    src, dst, held, sems = refs[:n], refs[n : 2 * n], refs[2 * n : 3 * n], refs[3 * n]
    come = [pltpu.make_async_copy(src[i], held[i], sems.at[0, i]) for i in range(n)]
    go = [pltpu.make_async_copy(held[i], dst[i], sems.at[1, i]) for i in range(n)]
    for copy in come:
        copy.start()
    for i in range(n):
        come[i].wait()
        go[i].start()
    for copy in go:
        copy.wait()


def copy_out(arrays):
    anywhere = pl.BlockSpec(memory_space=pl.ANY)
    n = len(arrays)
    return pl.pallas_call(
        functools.partial(copy_kernel, n),
        out_shape=tuple(jax.ShapeDtypeStruct(a.shape, a.dtype) for a in arrays),
        in_specs=[anywhere] * n,
        out_specs=(anywhere,) * n,
        scratch_shapes=[pltpu.VMEM(a.shape, a.dtype) for a in arrays]
        + [pltpu.SemaphoreType.DMA((2, n))],
        compiler_params=pltpu.CompilerParams(vmem_limit_bytes=VMEM_LIMIT),
    )(*arrays)


def on_device(
    queries, key_vectors, value_vectors, grad_output, pattern, lengths, widths, relative_bucket_bias,
    n_dp, n_ctx,
):
    tokens, width = queries.shape[1:]
    heads = relative_bucket_bias.shape[0]
    dim = width // heads
    vm = pl.BlockSpec(memory_space=pltpu.VMEM)
    hbm = pl.BlockSpec(memory_space=pl.ANY)
    dma = pltpu.SemaphoreType.DMA
    x = pltpu.VMEM((heads, 2, tokens, dim), BF16)
    half = pltpu.VMEM((heads, tokens, dim), BF16)
    acc = pltpu.VMEM((heads, tokens, dim), F32)
    pat = pltpu.VMEM((8, BLOCK), F32)
    per_head = dma((heads,))
    rows = jax.ShapeDtypeStruct(queries.shape, BF16)
    small = (lengths, widths, pattern, relative_bucket_bias)
    results = pl.pallas_call(
        functools.partial(kernel, n_dp, n_ctx, heads, tokens, dim ** (-0.5)),
        out_shape=(rows, rows, rows, jax.ShapeDtypeStruct(relative_bucket_bias.shape, F32)),
        in_specs=[hbm] * 8,
        out_specs=(vm,) * 4,
        scratch_shapes=[pltpu.SMEM(a.shape, a.dtype) for a in small]
        + [dma((len(small),))]
        + [per_head] * 4
        + [half, half, x, x, x, x, pat, pat, pat]
        + [half] * 6
        + [acc] * 3
        + [
            pltpu.VMEM((heads, 8, BLOCK), F32),
            pltpu.VMEM((2, 8, BLOCK), F32),
            pltpu.VMEM((n_ctx, 8, BLOCK), F32),
            pltpu.VMEM((n_dp, 8, BLOCK), F32),
            pltpu.VMEM((BLOCK, BLOCK), F32),
        ]
        + [per_head] * 6
        + [dma, dma, dma, dma]
        + [per_head] * 6
        + [dma((n_ctx,)), dma((n_ctx,)), dma((n_dp,)), dma((n_dp,))],
        compiler_params=pltpu.CompilerParams(
            collective_id=0, has_side_effects=True, vmem_limit_bytes=VMEM_LIMIT
        ),
    )(*small, queries, key_vectors, value_vectors, grad_output)
    return copy_out(results)


def solution(mesh):
    split = P("dp", "ctx", None)
    in_specs = (split,) * 5 + (P("dp", None), P("dp", None), P())
    body = functools.partial(on_device, n_dp=mesh.shape["dp"], n_ctx=mesh.shape["ctx"])
    return jax.shard_map(
        body, mesh=mesh, in_specs=in_specs, out_specs=(split,) * 3 + (P(),), check_vma=False
    )
```
